32 devices in a mesh: row: 8 (over y, x, core), col: 4 (over z).
Axes of the slice: x: 2, y: 2, z: 4, core: 2. Of those that a mesh axis runs over, the one named last changes fastest.
Arguments:
- values: float32 [8, 4, 36, 128, 128], P('row', 'col'), as said below
- block_ids: int32 [8, 4, 36, 2], P('row', 'col'), may hold values from -1 to 63, as said below
- coupled_rows: int32 [8, 4], replicated, may hold values from 0 to 63, as said below
Outputs:
- factored: float32 [8, 4, 36, 128, 128], P('row', 'col')
The draws below stay inside these ranges and needn't reach their ends.
Inputs may be any that keep to these rules, and one draw needn't show every extreme that they name: `coupled_rows`: row r holds 4 distinct block rows in increasing order, each equal to r modulo 8; every block row below 4 is among them. `block_ids`: the slots of device (r, c), in an order drawn from the seed, name each block (i, j) with i in row r of coupled_rows, j in a row r2 of coupled_rows with r2 equal to c modulo 4, and j <= i; and each diagonal block (i, i) of a block row i equal to r modulo 8 and to c modulo 4 that is not coupled; every other slot holds (-1, -1). No block is named twice. `values`: every stored diagonal block is symmetric, and the blocks of A in block rows and block columns below 4 form a symmetric positive definite matrix.
All inputs are finite; a program needn't handle non-finite values.
Results may differ from the reference program's by a relative error of at most 0.0003.
Values sent between devices are 32-bit elements; how exact they have to be, the bound alone decides.
No kernel may reach another device: no remote copies, remote signals or barrier semaphores. Data moves between devices by JAX's collectives and lax.ppermute only.
A program may use at most 128 MiB of HBM per device.

```python
import jax
import jax.numpy as jnp
from jax import lax

BLK = 128
BROWS = 8
SR = 4
PANELS = 4
N_ROW = 8
N_COL = 4


def layout(key):
    base = jax.random.fold_in(key, 11)
    row_keys = jax.random.split(jax.random.fold_in(base, 1), N_ROW)
    local_rows = jnp.arange(BROWS, dtype=jnp.int32)

    def shuffle_row(row_key, row_index):
        shuffled = jax.random.permutation(row_key, BROWS).astype(jnp.int32)
        zero_at = jnp.sum(jnp.where(shuffled == 0, local_rows, 0))
        forced = (row_index < PANELS) & (zero_at >= SR)
        last_row = shuffled[SR - 1]
        moved = jnp.where(forced & (local_rows == SR - 1), 0, shuffled)
        return jnp.where(forced & (local_rows == zero_at), last_row, moved)
    orders = jax.vmap(shuffle_row)(row_keys, jnp.arange(N_ROW, dtype=jnp.int32))
    row_index = jnp.arange(N_ROW, dtype=jnp.int32)[:, None]
    coupled = jnp.sort(orders[:, :SR], axis=1) * N_ROW + row_index
    spare = orders[:, SR:] * N_ROW + row_index
    groups = N_ROW // N_COL
    col_sets = jnp.transpose(coupled.reshape(groups, N_COL, SR), (1, 0, 2)).reshape(N_COL, groups * SR)
    left_ids = jnp.broadcast_to(coupled[:, None, :, None], (N_ROW, N_COL, SR, groups * SR))
    right_ids = jnp.broadcast_to(col_sets[None, :, None, :], (N_ROW, N_COL, SR, groups * SR))
    lower = right_ids <= left_ids
    pair_rows = jnp.where(lower, left_ids, -1).reshape(N_ROW, N_COL, SR * groups * SR)
    pair_cols = jnp.where(lower, right_ids, -1).reshape(N_ROW, N_COL, SR * groups * SR)
    holds = jnp.arange(N_ROW, dtype=jnp.int32)[:, None] % N_COL == jnp.arange(N_COL, dtype=jnp.int32)[None, :]
    spare_ids = jnp.where(holds[:, :, None], spare[:, None, :], -1)
    all_rows = jnp.concatenate([pair_rows, spare_ids], axis=2)
    all_cols = jnp.concatenate([pair_cols, spare_ids], axis=2)
    slot_count = all_rows.shape[2]
    slot_keys = jax.random.split(jax.random.fold_in(base, 2), N_ROW * N_COL)

    def slot_order(slot_key):
        return jax.random.permutation(slot_key, slot_count).astype(jnp.int32)
    reorder = jax.vmap(slot_order)(slot_keys).reshape(N_ROW, N_COL, slot_count)
    all_rows = jnp.take_along_axis(all_rows, reorder, axis=2)
    all_cols = jnp.take_along_axis(all_cols, reorder, axis=2)
    block_list = jnp.stack([all_rows, all_cols], axis=-1).astype(jnp.int32)
    return (coupled.astype(jnp.int32), block_list)


def draw_coupled_rows(key, part):
    coupled, block_list = layout(key)
    return coupled


def draw_block_ids(key, part):
    coupled, block_list = layout(key)
    return block_list


def draw_values(key, part):
    coupled, block_list = layout(key)
    key_lead, key_diagonal, key_blocks, key_filler = jax.random.split(jax.random.fold_in(key, 23), 4)
    total_rows = BROWS * N_ROW
    lead_order = PANELS * BLK
    panel_scale = 0.3
    lead_ints = jax.random.randint(key_lead, (lead_order, lead_order), -3, 4)
    lead_scale = 1.0 / (4.0 * lead_order)
    diagonal = jax.random.uniform(key_diagonal, (total_rows, BLK), jnp.float32, 0.25, 1.0)
    lead_float = lead_ints.astype(jnp.float32)
    leading = jnp.dot(lead_float, lead_float.T, precision=lax.Precision.HIGHEST) * lead_scale
    leading = jnp.transpose(leading.reshape(PANELS, BLK, PANELS, BLK), (0, 2, 1, 3))
    identity = jnp.eye(BLK, dtype=jnp.float32)
    slot_count = block_list.shape[2]
    filler = jax.random.normal(key_filler, (N_ROW * N_COL, slot_count, BLK, BLK), jnp.float32)
    flat_list = block_list.reshape(N_ROW * N_COL, slot_count, 2)

    def block_noise(block_row, block_col):
        block_key = jax.random.fold_in(jax.random.fold_in(key_blocks, block_row), block_col)
        fresh = jax.random.normal(block_key, (BLK, BLK), jnp.float32)
        return fresh

    def device_blocks(carried):
        device_ids, device_filler = carried
        rows_here = jnp.maximum(device_ids[:, 0], 0)
        cols_here = jnp.maximum(device_ids[:, 1], 0)
        noise = jax.vmap(block_noise)(rows_here, cols_here)
        same = (rows_here == cols_here)[:, None, None]
        symmetric = jnp.where(same, (noise + jnp.swapaxes(noise, 1, 2)) * 0.70710678, noise)
        diagonal_add = jnp.where(same, diagonal[rows_here][:, :, None] * identity[None], 0.0)
        lead_rows = jnp.minimum(rows_here, PANELS - 1)
        lead_cols = jnp.minimum(cols_here, PANELS - 1)
        lead_block = leading[lead_rows, lead_cols] + diagonal_add
        panel_block = panel_scale * noise
        trail_block = symmetric + diagonal_add
        is_lead = (rows_here < PANELS)[:, None, None]
        is_panel = (cols_here < PANELS)[:, None, None]
        stored = jnp.where(is_lead, lead_block, jnp.where(is_panel, panel_block, trail_block))
        return jnp.where((device_ids[:, 0] >= 0)[:, None, None], stored, device_filler)
    result = lax.map(device_blocks, (flat_list, filler))
    return result.reshape(N_ROW, N_COL, slot_count, BLK, BLK)


def setup_inputs(seed: int = 0) -> dict:
    seeds = jax.random.split(jax.random.key(seed), 4)
    return {
        "values": draw_values(jax.random.fold_in(seeds[3], 71), 0),
        "block_ids": draw_block_ids(jax.random.fold_in(seeds[3], 71), 0),
        "coupled_rows": draw_coupled_rows(jax.random.fold_in(seeds[3], 71), 0),
    }


exact_precision = lax.Precision.HIGHEST

def locate(wanted, known_rows):
    matched = wanted[:, None] == known_rows[None, :]
    places = jnp.arange(known_rows.shape[0], dtype=jnp.int32)
    found_at = jnp.sum(jnp.where(matched, places[None, :], 0), axis=1).astype(jnp.int32)
    return (found_at, jnp.any(matched, axis=1))

def reference(values, block_ids, coupled_rows):
    device_count = values.shape[0] * values.shape[1]
    slot_count = values.shape[2]
    block_size = values.shape[-1]
    state = values.reshape(device_count, slot_count, block_size, block_size)
    flat_ids = block_ids.reshape(device_count, slot_count, 2).astype(jnp.int32)
    row_ids = flat_ids[:, :, 0]
    col_ids = flat_ids[:, :, 1]
    members = coupled_rows.reshape(-1).astype(jnp.int32)
    member_count = members.shape[0]
    member_places = jnp.arange(member_count, dtype=jnp.int32)
    row_flat, row_found = locate(row_ids.reshape(-1), members)
    col_flat, col_found = locate(col_ids.reshape(-1), members)
    coupled_flat = row_found & col_found
    row_place = row_flat.reshape(device_count, slot_count)
    col_place = col_flat.reshape(device_count, slot_count)
    coupled = coupled_flat.reshape(device_count, slot_count)
    slot_numbers = jnp.arange(device_count * slot_count, dtype=jnp.int32)
    identity = jnp.eye(block_size, dtype=jnp.float32)
    for column in range(PANELS):
        flat_state = state.reshape(device_count * slot_count, block_size, block_size)
        in_column = coupled_flat & (col_ids.reshape(-1) == column)
        chosen = in_column[:, None] & (row_flat[:, None] == member_places[None, :])
        slot_of = jnp.sum(jnp.where(chosen, slot_numbers[:, None], 0), axis=0).astype(jnp.int32)
        present = jnp.any(chosen, axis=0)
        raw_panel = jnp.where(present[:, None, None], flat_state[slot_of], 0.0)
        pivot_at = jnp.argmax((members == column).astype(jnp.int32))
        pivot_factor = jnp.linalg.cholesky(raw_panel[pivot_at])
        inverse = jax.scipy.linalg.solve_triangular(pivot_factor, identity, lower=True)
        scaled = jnp.einsum('mab,cb->mac', raw_panel, inverse, precision=exact_precision)
        panel_blocks = jnp.where((members > column)[:, None, None], scaled, jnp.where((members == column)[:, None, None], pivot_factor[None], 0.0))

        def update_device(carried):
            device_values, device_rows, device_cols, device_col_ids, device_coupled = carried
            left_block = panel_blocks[device_rows]
            right_block = panel_blocks[device_cols]
            product = jnp.einsum('sab,scb->sac', left_block, right_block, precision=exact_precision)
            active = device_coupled & (device_col_ids > column)
            updated = device_values - jnp.where(active[:, None, None], product, 0.0)
            replace = device_coupled & (device_col_ids == column)
            return jnp.where(replace[:, None, None], left_block, updated)
        state = lax.map(update_device, (state, row_place, col_place, col_ids, coupled))
    state = jnp.where((row_ids >= 0)[:, :, None, None], state, 0.0)
    return state.reshape(values.shape)
```

```python
import functools

import jax
import jax.numpy as jnp
from jax import lax
from jax.experimental import pallas as pl
from jax.experimental.pallas import tpu as pltpu
from jax.sharding import PartitionSpec as P

PANELS = 4
GROUP = 32
SUB = 8
STRIPS = GROUP // SUB
F32 = jnp.float32
BF16 = jnp.bfloat16
HIGHEST = lax.Precision.HIGHEST
HBM = pl.BlockSpec(memory_space=pl.ANY)
SMEM = pl.BlockSpec(memory_space=pltpu.SMEM)
VMEM = pl.BlockSpec(memory_space=pltpu.VMEM)


def find(ids, rows, place, slots):
    me, column = lax.axis_index("row"), lax.axis_index("col")
    places = lax.broadcasted_iota(jnp.int32, (1, slots), 1)
    hit = (ids[1:2, :] == column) & (ids[0:1, :] == rows[place, me])
    return jnp.max(jnp.where(hit, places, -1))


def extract_kernel(col_devices, ids, rows, values, head, tail, table, sems):
    slots, count = values.shape[0], rows.shape[0]
    groups = rows.shape[1] // col_devices
    me = lax.axis_index("row")
    column = lax.axis_index("col")
    copies, present = [], []
    for place in range(count):
        found = find(ids, rows, place, slots)
        present.append(found >= 0)
        target = head.at[0] if place == 0 else tail.at[place - 1]
        copy = pltpu.make_async_copy(values.at[jnp.maximum(found, 0)], target, sems.at[place])
        copy.start()
        copies.append(copy)
    row_ids, col_ids = ids[0:1, :], ids[1:2, :]
    row_place = jnp.full((1, slots), -1, jnp.int32)
    col_place = jnp.full((1, slots), -1, jnp.int32)
    for place in range(count):
        row_place = jnp.where(row_ids == rows[place, me], place, row_place)
        for group in range(groups):
            known = rows[place, column + group * col_devices]
            col_place = jnp.where(col_ids == known, group * count + place, col_place)
    both = (row_place >= 0) & (col_place >= 0)
    kind = jnp.where(row_ids < 0, 0, jnp.where(both, jnp.where(col_ids < PANELS, 2, 3), 1))
    table[0:1, :] = kind
    table[1:2, :] = jnp.maximum(row_place, 0)
    table[2:3, :] = jnp.maximum(col_place, 0)
    for place, copy in enumerate(copies):
        copy.wait()
        if place == 0:
            head[0] = jnp.where(present[place], head[0], 0.0)
        else:
            tail[place - 1] = jnp.where(present[place], tail[place - 1], 0.0)


def extract(ids, rows, values, col_devices):
    slots, size, _ = values.shape
    count = rows.shape[0]
    return pl.pallas_call(
        functools.partial(extract_kernel, col_devices),
        name="extract",
        in_specs=[VMEM, SMEM, HBM],
        out_specs=[VMEM, VMEM, VMEM],
        out_shape=[
            jax.ShapeDtypeStruct((1, size, size), F32),
            jax.ShapeDtypeStruct((count - 1, size, size), F32),
            jax.ShapeDtypeStruct((3, slots), jnp.int32),
        ],
        scratch_shapes=[pltpu.SemaphoreType.DMA((count,))],
    )(ids, rows, values)


def one_row(strip, place):
    return jnp.broadcast_to(strip[place : place + 1, :], strip.shape)


def eliminate(upper, extra, diagonal):
    width = upper[0].shape[1]
    sublane = lax.broadcasted_iota(jnp.int32, (SUB, width), 0)
    cols = [
        [
            jnp.broadcast_to(diagonal[q][:, t : t + 1], (SUB, width)) if q >= t // SUB else None
            for q in range(STRIPS)
        ]
        for t in range(GROUP)
    ]
    scale = [jnp.zeros((SUB, width), F32)] * STRIPS
    for t in range(GROUP):
        strip, place = divmod(t, SUB)
        pivot = one_row(cols[t][strip], place)
        reciprocal = 1.0 / pivot
        scale[strip] = jnp.where(sublane == place, lax.rsqrt(pivot), scale[strip])
        factor = {q: cols[t][q] * reciprocal for q in range(strip, STRIPS)}
        factor[strip] = jnp.where(sublane > place, factor[strip], 0.0)
        for u in range(t + 1, GROUP):
            entry = one_row(cols[t][u // SUB], u % SUB)
            for q in range(u // SUB, STRIPS):
                cols[u][q] = cols[u][q] - factor[q] * entry
        pivot_upper = one_row(upper[strip], place)
        pivot_extra = one_row(extra[strip], place)
        for q in range(strip, STRIPS):
            upper[q] = upper[q] - factor[q] * pivot_upper
            extra[q] = extra[q] - factor[q] * pivot_extra
    upper = jnp.concatenate([upper[q] * scale[q] for q in range(STRIPS)], axis=0)
    extra = jnp.concatenate([extra[q] * scale[q] for q in range(STRIPS)], axis=0)
    return upper, extra


def exact(a, b):
    return jnp.dot(a, b, precision=HIGHEST, preferred_element_type=F32)


def exact_t(a, b):
    return lax.dot_general(
        a, b, (((1,), (1,)), ((), ())), precision=HIGHEST, preferred_element_type=F32
    )


def factor_block(block, work, extra_work):
    size = block.shape[0]
    row_place = lax.broadcasted_iota(jnp.int32, (size, size), 0)
    col_place = lax.broadcasted_iota(jnp.int32, (size, size), 1)
    work[...] = block
    extra_work[...] = jnp.where(row_place == col_place, 1.0, 0.0)
    uppers, extras = [], []
    for start in range(0, size, GROUP):
        strips = [pl.ds(start + q * SUB, SUB) for q in range(STRIPS)]
        upper = [work[s, :] for s in strips]
        extra = [extra_work[s, :] for s in strips]
        diagonal = [strip[:, start : start + GROUP] for strip in upper]
        upper, extra = eliminate(upper, extra, diagonal)
        uppers.append(upper)
        extras.append(extra)
        end = start + GROUP
        if end < size:
            left = upper[:, end:].T
            work[end:, :] = work[end:, :] - exact(left, upper)
            extra_work[end:, :] = extra_work[end:, :] - exact(left, extra)
    upper = jnp.concatenate(uppers, axis=0)
    inverse = jnp.where(row_place >= col_place, jnp.concatenate(extras, axis=0), 0.0)
    return jnp.where(row_place <= col_place, upper, 0.0), inverse


def halves(x):
    high = x.astype(BF16)
    return high, (x - high.astype(F32)).astype(BF16)


def lead_kernel(near, across, factor, inv_hi, inv_lo, lead, inverse, work, extra_work):
    size = near.shape[-1]
    me = lax.axis_index("row")
    column = lax.axis_index("col")
    for row in range(PANELS):
        for col in range(row + 1):
            flip_x = ((me // 2) % 2) ^ (row // 2)
            flip_core = (me % 2) ^ (row % 2)
            place = column ^ col

            @pl.when(flip_core == 0)
            def _():
                lead[row, col] = near[flip_x, place]

            @pl.when(flip_core == 1)
            def _():
                lead[row, col] = across[flip_x, place]

    zero = jnp.zeros((size, size), F32)
    for k in range(PANELS):
        upper, inv = factor_block(lead[k, k], work, extra_work)
        lead[k, k] = upper.T
        for i in range(k + 1, PANELS):
            lead[i, k] = exact_t(lead[i, k], inv)
        for i in range(k + 1, PANELS):
            for j in range(k + 1, i + 1):
                lead[i, j] = lead[i, j] - exact_t(lead[i, k], lead[j, k])
        for j in range(PANELS):
            rows, cols = slice(k * size, (k + 1) * size), slice(j * size, (j + 1) * size)
            if j > k:
                inverse[rows, cols] = zero
            elif j == k:
                inverse[rows, cols] = inv
            else:
                total = zero
                for m in range(j, k):
                    total = total + exact(
                        lead[k, m], inverse[m * size : (m + 1) * size, j * size : (j + 1) * size]
                    )
                inverse[rows, cols] = -exact(inv, total)
    inv_hi[...], inv_lo[...] = halves(inverse[...])
    factor[...] = lead[jnp.minimum(me, PANELS - 1), jnp.minimum(column, PANELS - 1)]


def factor_lead(near, across):
    size = near.shape[-1]
    width = PANELS * size
    return pl.pallas_call(
        lead_kernel,
        name="factor_lead",
        in_specs=[VMEM, VMEM],
        out_specs=[VMEM, VMEM, VMEM],
        out_shape=[
            jax.ShapeDtypeStruct((size, size), F32),
            jax.ShapeDtypeStruct((width, width), BF16),
            jax.ShapeDtypeStruct((width, width), BF16),
        ],
        scratch_shapes=[
            pltpu.VMEM((PANELS, PANELS, size, size), F32),
            pltpu.VMEM((width, width), F32),
            pltpu.VMEM((size, size), F32),
            pltpu.VMEM((size, size), F32),
        ],
        compiler_params=pltpu.CompilerParams(vmem_limit_bytes=16 * 2**20),
        cost_estimate=pl.CostEstimate(flops=2**34, bytes_accessed=2**25, transcendentals=0),
    )(near, across)


def dot3_t(a, b):
    dims = (((1,), (1,)), ((), ()))
    dot = functools.partial(lax.dot_general, dimension_numbers=dims, preferred_element_type=F32)
    return dot(a[0], b[0]) + (dot(a[0], b[1]) + dot(a[1], b[0]))


def update_kernel(plan, table, *refs):
    groups, count, col_devices = plan
    refs = list(refs)
    heads = [refs.pop(0) for _ in range(col_devices)]
    tails = [refs.pop(0) for _ in range(col_devices)]
    others = [None, None] + [refs.pop(0) for _ in range(2, col_devices)]
    near = [refs.pop(0) for _ in range(groups)]
    across = [refs.pop(0) for _ in range(groups)]
    factor, inv_hi, inv_lo, values, out = [refs.pop(0) for _ in range(5)]
    raw, high, low, product, slots_in, sems, io_sems = refs
    slots, size, _ = values.shape
    own_rows = count * size
    far_rows = groups * own_rows
    me = lax.axis_index("row")
    column = lax.axis_index("col")

    load = pltpu.make_async_copy(values, slots_in, io_sems.at[0])
    load.start()
    same_core = ((me ^ column) % 2) == 0
    owner = ((me ^ column) % col_devices) == 0
    for p in range(col_devices):
        col = column ^ p

        @pl.when(col < PANELS)
        def _():
            lanes = pl.ds(pl.multiple_of(jnp.minimum(col, PANELS - 1) * size, size), size)
            for place in range(count):
                target = raw.at[pl.ds(place * size, size), lanes]
                if place == 0 or p < 2:
                    source = heads[p].at[0] if place == 0 else tails[p].at[place - 1]
                    pltpu.make_async_copy(source, target, sems.at[0]).start()
                    continue

                @pl.when(owner)
                def _():
                    pltpu.make_async_copy(tails[p].at[place - 1], target, sems.at[0]).start()

                @pl.when(jnp.logical_not(owner))
                def _():
                    pltpu.make_async_copy(others[p].at[place - 1], target, sems.at[0]).start()

            for q in range(groups):
                group = (me // col_devices) ^ q
                for place in range(count):
                    block = p * count + place
                    rows = pl.ds(
                        pl.multiple_of(own_rows + (group * count + place) * size, size), size
                    )

                    @pl.when(same_core)
                    def _():
                        pltpu.make_async_copy(
                            near[q].at[block], raw.at[rows, lanes], sems.at[1]
                        ).start()

                    @pl.when(jnp.logical_not(same_core))
                    def _():
                        pltpu.make_async_copy(
                            across[q].at[block], raw.at[rows, lanes], sems.at[1]
                        ).start()

    half = PANELS * size // 2
    for part in range(groups + 1):
        if part < 2:
            arrived = raw.at[:own_rows, :] if part == 0 else raw.at[own_rows:, :]
            pltpu.make_async_copy(arrived, arrived, sems.at[part]).wait()
        rows = pl.ds(part * own_rows, own_rows)
        hi, lo = halves(raw[rows, :])
        first = dot3_t(
            (hi[:, :half], lo[:, :half]), (inv_hi[:half, :half], inv_lo[:half, :half])
        )
        second = dot3_t((hi, lo), (inv_hi[half:, :], inv_lo[half:, :]))
        if part == 0:
            raw[rows, :half], raw[rows, half:] = first, second
        high[rows, :half], low[rows, :half] = halves(first)
        high[rows, half:], low[rows, half:] = halves(second)
    load.wait()
    own = pl.ds(0, own_rows)
    for start in range(0, far_rows, 2 * size):
        rows = pl.ds(own_rows + start, 2 * size)
        result = dot3_t((high[own, :], low[own, :]), (high[rows, :], low[rows, :]))
        for place in range(count):
            for side in range(2):
                product[place, start // size + side] = result[
                    place * size : (place + 1) * size, side * size : (side + 1) * size
                ]
    lead_row = me < PANELS
    lead_col = jnp.minimum(column, PANELS - 1)
    lanes = pl.ds(pl.multiple_of(lead_col * size, size), size)

    def finish(slot, carry):
        kind, row, col = table[0, slot], table[1, slot], table[2, slot]

        @pl.when(kind == 0)
        def _():
            slots_in[slot] = jnp.zeros((size, size), F32)

        @pl.when(kind == 3)
        def _():
            slots_in[slot] = slots_in[slot] - product[row, col]

        @pl.when((kind == 2) & lead_row & (row == 0))
        def _():
            slots_in[slot] = factor[...]

        @pl.when((kind == 2) & jnp.logical_not(lead_row & (row == 0)))
        def _():
            slots_in[slot] = raw[pl.ds(pl.multiple_of(row * size, size), size), lanes]

        pltpu.make_async_copy(slots_in.at[slot], out.at[slot], io_sems.at[1]).start()
        return carry

    lax.fori_loop(0, slots, finish, 0)
    pltpu.make_async_copy(slots_in, out, io_sems.at[1]).wait()


def update(table, heads, tails, others, near, across, solved_lead, values, col_devices):
    slots, size, _ = values.shape
    groups, count = len(near), tails[0].shape[0] + 1
    flat = [*heads, *tails, *others, *near, *across]
    width = PANELS * size
    rows = (groups + 1) * count * size
    return pl.pallas_call(
        functools.partial(update_kernel, (groups, count, col_devices)),
        name="update",
        in_specs=[SMEM] + [HBM] * len(flat) + [VMEM, VMEM, VMEM, HBM],
        out_specs=HBM,
        out_shape=jax.ShapeDtypeStruct(values.shape, F32),
        scratch_shapes=[
            pltpu.VMEM((rows, width), F32),
            pltpu.VMEM((rows, width), BF16),
            pltpu.VMEM((rows, width), BF16),
            pltpu.VMEM((count, groups * count, size, size), F32),
            pltpu.VMEM((slots, size, size), F32),
            pltpu.SemaphoreType.DMA((2,)),
            pltpu.SemaphoreType.DMA((2,)),
        ],
        compiler_params=pltpu.CompilerParams(vmem_limit_bytes=24 * 2**20),
    )(table, *flat, *solved_lead, values)


def pack_kernel(pieces, *refs):
    heads, tails = refs[:pieces], refs[pieces : 2 * pieces]
    packed, sem = refs[-2:]
    count = packed.shape[0] // pieces
    for p in range(pieces):
        at = p * count
        pltpu.make_async_copy(heads[p], packed.at[at : at + 1], sem).start()
        pltpu.make_async_copy(tails[p], packed.at[at + 1 : at + count], sem).start()
    pltpu.make_async_copy(packed, packed, sem).wait()


def pack(heads, tails):
    size = heads[0].shape[-1]
    blocks = sum(x.shape[0] for x in (*heads, *tails))
    operands = [*heads, *tails]
    return pl.pallas_call(
        functools.partial(pack_kernel, len(heads)),
        name="pack",
        in_specs=[HBM] * len(operands),
        out_specs=VMEM,
        out_shape=jax.ShapeDtypeStruct((blocks, size, size), F32),
        scratch_shapes=[pltpu.SemaphoreType.DMA],
    )(*operands)


def body(values, block_ids, coupled_rows):
    row_devices, col_devices = lax.axis_size("row"), lax.axis_size("col")
    every_row, every_col = range(row_devices), range(col_devices)
    groups = row_devices // col_devices
    me, column = lax.axis_index("row"), lax.axis_index("col")
    slot_values = values[0, 0]
    rows = coupled_rows.T

    def send(x, flip, keep=lambda r, c: True):
        pairs = [
            (r * col_devices + c, (r ^ flip) * col_devices + c)
            for r in every_row
            for c in every_col
            if keep(r, c)
        ]
        return lax.ppermute(x, ("row", "col"), pairs)

    def over_col(x, flips, keep=lambda r, c: True):
        got = []
        for p in flips:
            pairs = [
                (r * col_devices + c, r * col_devices + (c ^ p))
                for r in every_row
                for c in range(PANELS)
                if keep(r, c ^ p)
            ]
            got.append(lax.ppermute(x, ("row", "col"), pairs))
        return got

    def owner(r, c):
        return (r ^ c) % col_devices == 0

    head, tail, table = extract(block_ids[0, 0].T, rows, slot_values, col_devices)
    heads = [head, *over_col(head, range(1, col_devices))]
    tails = [tail, *over_col(tail, [1]), *over_col(tail, range(2, col_devices), owner)]

    mine = jnp.concatenate(heads, axis=0)
    flips = [high + low for high in range(0, row_devices, PANELS) for low in (0, 2)]
    arrived = [mine if flip == 0 else send(mine, flip, lambda r, c: r < PANELS) for flip in flips]
    arrived, tails = lax.optimization_barrier((arrived, tails))
    same, beside = arrived[:2]
    for flip, got, got_beside in zip(flips[2::2], arrived[2::2], arrived[3::2]):
        here = (me // PANELS) * PANELS == flip
        same, beside = jnp.where(here, got, same), jnp.where(here, got_beside, beside)
    near_lead = jnp.stack([same, beside])
    across_lead = send(near_lead, 1)
    solved_lead = factor_lead(near_lead, across_lead)

    owned = pack(heads, tails)
    others = over_col(tail, range(2, col_devices), lambda r, c: not owner(r, c))
    flips = [q * col_devices + low for q in range(groups) for low in range(0, col_devices, 2)]
    far = [owned if flip == 0 else send(owned, flip, owner) for flip in flips]
    far, others, solved_lead = lax.optimization_barrier((far, others, solved_lead))
    near, across = [], []
    for q in range(groups):
        part = None
        for flip, got in zip(flips, far):
            if flip // col_devices == q:
                here = (me ^ column) % col_devices // 2 * 2 == flip % col_devices
                part = got if part is None else jnp.where(here, got, part)
        near.append(part)
        across.append(send(part, 1, lambda r, c: (r ^ c) % 2 == 0))

    result = update(
        table, heads, tails, others, near, across, solved_lead, slot_values, col_devices
    )
    return result[None, None]


def solution(mesh):
    placed = (P("row", "col", None, None, None), P("row", "col", None, None), P())
    return jax.shard_map(
        body,
        mesh=mesh,
        in_specs=placed,
        out_specs=P("row", "col", None, None, None),
        check_vma=False,
    )
```

```python
import functools

import jax
import jax.numpy as jnp
from jax import lax
from jax.experimental import pallas as pl
from jax.experimental.pallas import tpu as pltpu
from jax.sharding import PartitionSpec as P

PANELS = 4
FIRST = 3
GROUP = 32
CHUNK = 16
SUB = 8
STRIPS = GROUP // SUB
F32 = jnp.float32
BF16 = jnp.bfloat16
HIGHEST = lax.Precision.HIGHEST
HBM = pl.BlockSpec(memory_space=pl.ANY)
SMEM = pl.BlockSpec(memory_space=pltpu.SMEM)
VMEM = pl.BlockSpec(memory_space=pltpu.VMEM)


def find(ids, rows, place, slots):
    me, column = lax.axis_index("row"), lax.axis_index("col")
    places = lax.broadcasted_iota(jnp.int32, (1, slots), 1)
    hit = (ids[1:2, :] == column) & (ids[0:1, :] == rows[place, me])
    return jnp.max(jnp.where(hit, places, -1))


def extract_kernel(col_devices, ids, rows, values, panel, head, table, sems):
    slots, count = values.shape[0], rows.shape[0]
    groups = rows.shape[1] // col_devices
    me = lax.axis_index("row")
    column = lax.axis_index("col")
    copies, present = [], []
    for place in range(count):
        found = find(ids, rows, place, slots)
        present.append(found >= 0)
        copy = pltpu.make_async_copy(
            values.at[jnp.maximum(found, 0)], panel.at[place], sems.at[place]
        )
        copy.start()
        copies.append(copy)
    row_ids, col_ids = ids[0:1, :], ids[1:2, :]
    row_place = jnp.full((1, slots), -1, jnp.int32)
    col_place = jnp.full((1, slots), -1, jnp.int32)
    for place in range(count):
        row_place = jnp.where(row_ids == rows[place, me], place, row_place)
        for group in range(groups):
            known = rows[place, column + group * col_devices]
            col_place = jnp.where(col_ids == known, group * count + place, col_place)
    both = (row_place >= 0) & (col_place >= 0)
    kind = jnp.where(row_ids < 0, 0, jnp.where(both, jnp.where(col_ids < PANELS, 2, 3), 1))
    table[0:1, :] = kind
    table[1:2, :] = jnp.maximum(row_place, 0)
    table[2:3, :] = jnp.maximum(col_place, 0)
    for place, copy in enumerate(copies):
        copy.wait()
        block = jnp.where(present[place], panel[place], 0.0)
        panel[place] = block
        if place == 0:
            head[0] = block


def extract(ids, rows, values, col_devices):
    slots, size, _ = values.shape
    count = rows.shape[0]
    return pl.pallas_call(
        functools.partial(extract_kernel, col_devices),
        name="extract",
        in_specs=[VMEM, SMEM, HBM],
        out_specs=[VMEM, VMEM, VMEM],
        out_shape=[
            jax.ShapeDtypeStruct((count, size, size), F32),
            jax.ShapeDtypeStruct((1, size, size), F32),
            jax.ShapeDtypeStruct((3, slots), jnp.int32),
        ],
        scratch_shapes=[pltpu.SemaphoreType.DMA((count,))],
    )(ids, rows, values)


def one_row(strip, place):
    return jnp.broadcast_to(strip[place : place + 1, :], strip.shape)


def eliminate(upper, extra, start):
    width = upper[0].shape[1]
    sublane = lax.broadcasted_iota(jnp.int32, (SUB, width), 0)
    scale = [jnp.zeros((SUB, width), F32)] * STRIPS
    for first in range(0, GROUP, CHUNK):
        chunk = range(first, first + CHUNK)
        cols = {
            t: {
                q: jnp.broadcast_to(upper[q][:, start + t : start + t + 1], (SUB, width))
                for q in range(t // SUB, STRIPS)
            }
            for t in chunk
        }
        for t in chunk:
            strip, place = divmod(t, SUB)
            pivot = one_row(cols[t][strip], place)
            reciprocal = 1.0 / pivot
            scale[strip] = jnp.where(sublane == place, lax.rsqrt(pivot), scale[strip])
            factor = {q: cols[t][q] * reciprocal for q in range(strip, STRIPS)}
            factor[strip] = jnp.where(sublane > place, factor[strip], 0.0)
            for u in chunk[t + 1 - first :]:
                entry = one_row(cols[t][u // SUB], u % SUB)
                for q in range(u // SUB, STRIPS):
                    cols[u][q] = cols[u][q] - factor[q] * entry
            pivot_upper = one_row(upper[strip], place)
            pivot_extra = one_row(extra[strip], place)
            for q in range(strip, STRIPS):
                upper[q] = upper[q] - factor[q] * pivot_upper
                extra[q] = extra[q] - factor[q] * pivot_extra
    upper = jnp.concatenate([upper[q] * scale[q] for q in range(STRIPS)], axis=0)
    extra = jnp.concatenate([extra[q] * scale[q] for q in range(STRIPS)], axis=0)
    return upper, extra


def exact(a, b):
    return jnp.dot(a, b, precision=HIGHEST, preferred_element_type=F32)


def exact_t(a, b):
    return lax.dot_general(
        a, b, (((1,), (1,)), ((), ())), precision=HIGHEST, preferred_element_type=F32
    )


def factor_block(block, work, extra_work):
    size = block.shape[0]
    row_place = lax.broadcasted_iota(jnp.int32, (size, size), 0)
    col_place = lax.broadcasted_iota(jnp.int32, (size, size), 1)
    work[...] = block
    extra_work[...] = jnp.where(row_place == col_place, 1.0, 0.0)
    uppers, extras = [], []
    for start in range(0, size, GROUP):
        strips = [pl.ds(start + q * SUB, SUB) for q in range(STRIPS)]
        upper = [work[s, :] for s in strips]
        extra = [extra_work[s, :] for s in strips]
        upper, extra = eliminate(upper, extra, start)
        uppers.append(upper)
        extras.append(extra)
        end = start + GROUP
        if end < size:
            left = upper[:, end:].T
            work[end:, :] = work[end:, :] - exact(left, upper)
            extra_work[end:, :] = extra_work[end:, :] - exact(left, extra)
    upper = jnp.concatenate(uppers, axis=0)
    inverse = jnp.where(row_place >= col_place, jnp.concatenate(extras, axis=0), 0.0)
    return jnp.where(row_place <= col_place, upper, 0.0), inverse


def halves(x):
    high = x.astype(BF16)
    return high, (x - high.astype(F32)).astype(BF16)


def at(row, col):
    return row * (row + 1) // 2 + col


def factor_steps(steps, lead, inverse, work, extra_work):
    for k in steps:
        upper, inv = factor_block(lead[at(k, k)], work, extra_work)
        lead[at(k, k)] = upper.T
        for i in range(k + 1, PANELS):
            lead[at(i, k)] = exact_t(lead[at(i, k)], inv)
        for i in range(k + 1, PANELS):
            for j in range(k + 1, i + 1):
                lead[at(i, j)] = lead[at(i, j)] - exact_t(lead[at(i, k)], lead[at(j, k)])
        inverse[at(k, k)] = inv
        for j in range(k):
            total = exact(lead[at(k, j)], inverse[at(j, j)])
            for m in range(j + 1, k):
                total = total + exact(lead[at(k, m)], inverse[at(m, j)])
            inverse[at(k, j)] = -exact(inv, total)


def first_kernel(near, across, lead, inverse, work, extra_work):
    me = lax.axis_index("row")
    column = lax.axis_index("col")
    for row in range(PANELS):
        for col in range(row + 1):
            flip_x = ((me // 2) % 2) ^ (row // 2)
            flip_core = (me % 2) ^ (row % 2)
            place = column ^ col

            @pl.when(flip_core == 0)
            def _():
                lead[at(row, col)] = near[flip_x, place]

            @pl.when(flip_core == 1)
            def _():
                lead[at(row, col)] = across[flip_x, place]

    factor_steps(range(FIRST), lead, inverse, work, extra_work)


def second_kernel(
    lead_in, inverse_in, factor, inv_hi, inv_lo, lead, inverse, work, extra_work
):
    size = work.shape[0]
    done = at(FIRST, 0)
    lead[...] = lead_in[...]
    inverse[:done] = inverse_in[...]
    factor_steps(range(FIRST, PANELS), lead, inverse, work, extra_work)
    zero = jnp.zeros((size, size), BF16)
    for i in range(PANELS):
        for j in range(PANELS):
            rows, cols = slice(i * size, (i + 1) * size), slice(j * size, (j + 1) * size)
            hi, lo = halves(inverse[at(i, j)]) if j <= i else (zero, zero)
            inv_hi[rows, cols], inv_lo[rows, cols] = hi, lo
    row = jnp.minimum(lax.axis_index("row"), PANELS - 1)
    factor[...] = lead[at(row, jnp.minimum(lax.axis_index("col"), row))]


FACTOR_COST = pl.CostEstimate(flops=2**33, bytes_accessed=2**24, transcendentals=0)


def factor_first(near, across):
    size = near.shape[-1]
    return pl.pallas_call(
        first_kernel,
        name="factor_first",
        in_specs=[VMEM, VMEM],
        out_specs=[VMEM, VMEM],
        out_shape=[
            jax.ShapeDtypeStruct((at(PANELS, 0), size, size), F32),
            jax.ShapeDtypeStruct((at(FIRST, 0), size, size), F32),
        ],
        scratch_shapes=[pltpu.VMEM((size, size), F32), pltpu.VMEM((size, size), F32)],
        compiler_params=pltpu.CompilerParams(vmem_limit_bytes=16 * 2**20),
        cost_estimate=FACTOR_COST,
    )(near, across)


def factor_second(lead, inverse):
    size = lead.shape[-1]
    width = PANELS * size
    return pl.pallas_call(
        second_kernel,
        name="factor_second",
        in_specs=[VMEM, VMEM],
        out_specs=[VMEM, VMEM, VMEM],
        out_shape=[
            jax.ShapeDtypeStruct((size, size), F32),
            jax.ShapeDtypeStruct((width, width), BF16),
            jax.ShapeDtypeStruct((width, width), BF16),
        ],
        scratch_shapes=[
            pltpu.VMEM((at(PANELS, 0), size, size), F32),
            pltpu.VMEM((at(PANELS, 0), size, size), F32),
            pltpu.VMEM((size, size), F32),
            pltpu.VMEM((size, size), F32),
        ],
        compiler_params=pltpu.CompilerParams(vmem_limit_bytes=16 * 2**20),
        cost_estimate=FACTOR_COST,
    )(lead, inverse)


def dot3_t(a, b):
    dims = (((1,), (1,)), ((), ()))
    dot = functools.partial(lax.dot_general, dimension_numbers=dims, preferred_element_type=F32)
    return dot(a[0], b[0]) + (dot(a[0], b[1]) + dot(a[1], b[0]))


def spread(column, place):
    return place ^ (2 * (column % 2))


def update_kernel(plan, table, *refs):
    row_devices, count, col_devices = plan
    groups = row_devices // col_devices
    refs = list(refs)
    panels = [refs.pop(0) for _ in range(col_devices)]
    near = [refs.pop(0) for _ in range(row_devices // 2)]
    across = refs.pop(0)
    factor, inv_hi, inv_lo, values, out = [refs.pop(0) for _ in range(5)]
    raw, high, low, product, column_blocks, slots_in, sems, io_sems = refs
    slots, size, _ = values.shape
    own_rows = count * size
    far_rows = groups * own_rows
    me = lax.axis_index("row")
    column = lax.axis_index("col")

    load = pltpu.make_async_copy(values, slots_in, io_sems.at[0])
    load.start()
    twice = (me ^ column) % col_devices == 0
    for p in range(col_devices):
        col = column ^ p

        @pl.when((col < PANELS) & jnp.logical_not(twice))
        def _():
            lanes = pl.ds(pl.multiple_of(jnp.minimum(col, PANELS - 1) * size, size), size)
            for place in range(count):
                pltpu.make_async_copy(
                    panels[p].at[place], raw.at[pl.ds(place * size, size), lanes], sems.at[0]
                ).start()

    for flip in range(row_devices):
        holder = me ^ flip
        group, col = holder // col_devices, spread(column, holder % col_devices)

        @pl.when(col < PANELS)
        def _():
            lanes = pl.ds(pl.multiple_of(jnp.minimum(col, PANELS - 1) * size, size), size)
            for place in range(count):
                if flip % 2 == 0:
                    source = near[flip // 2].at[place]
                else:
                    source = across.at[flip // 2 * count + place]
                start = pl.multiple_of(own_rows + (group * count + place) * size, size)
                pltpu.make_async_copy(
                    source, raw.at[pl.ds(start, size), lanes], sems.at[1]
                ).start()

                @pl.when(twice & (group == me // col_devices))
                def _():
                    pltpu.make_async_copy(
                        source, raw.at[pl.ds(place * size, size), lanes], sems.at[0]
                    ).start()

    half = PANELS * size // 2
    for part in range(groups + 1):
        if part < 2:
            arrived = raw.at[:own_rows, :] if part == 0 else raw.at[own_rows:, :]
            pltpu.make_async_copy(arrived, arrived, sems.at[part]).wait()
        rows = pl.ds(part * own_rows, own_rows)
        hi, lo = halves(raw[rows, :])
        first = dot3_t(
            (hi[:, :half], lo[:, :half]), (inv_hi[:half, :half], inv_lo[:half, :half])
        )
        second = dot3_t((hi, lo), (inv_hi[half:, :], inv_lo[half:, :]))
        if part == 0:
            raw[rows, :half], raw[rows, half:] = first, second
        high[rows, :half], low[rows, :half] = halves(first)
        high[rows, half:], low[rows, half:] = halves(second)
    load.wait()
    own = pl.ds(0, own_rows)
    for start in range(0, far_rows, 2 * size):
        rows = pl.ds(own_rows + start, 2 * size)
        result = dot3_t((high[own, :], low[own, :]), (high[rows, :], low[rows, :]))
        for place in range(count):
            for side in range(2):
                product[place, start // size + side] = result[
                    place * size : (place + 1) * size, side * size : (side + 1) * size
                ]
    lanes = pl.ds(pl.multiple_of(jnp.minimum(column, PANELS - 1) * size, size), size)
    for place in range(count):
        solved_block = raw[place * size : (place + 1) * size, lanes]
        if place == 0:
            solved_block = jnp.where(me < PANELS, factor[...], solved_block)
        column_blocks[place] = solved_block

    def finish(slot, carry):
        kind, row, col = table[0, slot], table[1, slot], table[2, slot]
        old = slots_in[slot]
        new = jnp.where(kind == 3, old - product[row, col], jnp.where(kind == 1, old, 0.0))
        slots_in[slot] = jnp.where(kind == 2, column_blocks[row], new)
        pltpu.make_async_copy(slots_in.at[slot], out.at[slot], io_sems.at[1]).start()
        return carry

    lax.fori_loop(0, slots, finish, 0, unroll=4)
    pltpu.make_async_copy(slots_in, out, io_sems.at[1]).wait()


def update(table, panels, near, across, solved_lead, values, row_devices):
    slots, size, _ = values.shape
    col_devices, count = len(panels), panels[0].shape[0]
    groups = row_devices // col_devices
    flat = [*panels, *near, across]
    width = PANELS * size
    rows = (groups + 1) * count * size
    return pl.pallas_call(
        functools.partial(update_kernel, (row_devices, count, col_devices)),
        name="update",
        in_specs=[SMEM] + [HBM] * len(flat) + [VMEM, VMEM, VMEM, HBM],
        out_specs=HBM,
        out_shape=jax.ShapeDtypeStruct(values.shape, F32),
        scratch_shapes=[
            pltpu.VMEM((rows, width), F32),
            pltpu.VMEM((rows, width), BF16),
            pltpu.VMEM((rows, width), BF16),
            pltpu.VMEM((count, groups * count, size, size), F32),
            pltpu.VMEM((count, size, size), F32),
            pltpu.VMEM((slots, size, size), F32),
            pltpu.SemaphoreType.DMA((2,)),
            pltpu.SemaphoreType.DMA((2,)),
        ],
        compiler_params=pltpu.CompilerParams(vmem_limit_bytes=24 * 2**20),
    )(table, *flat, *solved_lead, values)


def body(values, block_ids, coupled_rows):
    row_devices, col_devices = lax.axis_size("row"), lax.axis_size("col")
    every_row, every_col = range(row_devices), range(col_devices)
    me = lax.axis_index("row")
    slot_values = values[0, 0]
    rows = coupled_rows.T

    def send(x, flip, keep=lambda r, c: True):
        pairs = [
            (r * col_devices + c, (r ^ flip) * col_devices + c)
            for r in every_row
            for c in every_col
            if keep(r, c)
        ]
        return lax.ppermute(x, ("row", "col"), pairs)

    def over_col(x, keep=lambda r, c: True):
        got = [x]
        for p in range(1, col_devices):
            pairs = [
                (r * col_devices + c, r * col_devices + (c ^ p))
                for r in every_row
                for c in range(PANELS)
                if keep(r, c ^ p)
            ]
            got.append(lax.ppermute(x, ("row", "col"), pairs))
        return got

    panel, head, table = extract(block_ids[0, 0].T, rows, slot_values, col_devices)

    block = jnp.where(me < PANELS, head, 0.0)
    step = PANELS
    while step < row_devices:
        block = block + send(block, step, lambda r, c: r < step)
        step *= 2
    blocks = over_col(block)

    pairs = [
        ((q + a) * col_devices + b, (q + spread(a, b)) * col_devices + a)
        for q in range(0, row_devices, col_devices)
        for a in every_col
        for b in range(PANELS)
    ]
    blocks, panel = lax.optimization_barrier((blocks, panel))
    turned = lax.ppermute(panel, ("row", "col"), pairs)

    panels = over_col(panel, lambda r, c: (r ^ c) % col_devices != 0)

    mine = jnp.concatenate(blocks, axis=0)
    beside, turned, panels[1] = lax.optimization_barrier((send(mine, 2), turned, panels[1]))
    near_lead = jnp.stack([mine, beside])
    across_lead = send(near_lead, 1)
    near = [turned if flip == 0 else send(turned, flip) for flip in range(0, row_devices, 2)]
    begun = factor_first(near_lead, across_lead)
    near, panels[2:], begun = lax.optimization_barrier((near, panels[2:], begun))
    across = send(jnp.concatenate(near, axis=0), 1)
    solved_lead = factor_second(*begun)

    result = update(table, panels, near, across, solved_lead, slot_values, row_devices)
    return result[None, None]


def solution(mesh):
    placed = (P("row", "col", None, None, None), P("row", "col", None, None), P())
    return jax.shard_map(
        body,
        mesh=mesh,
        in_specs=placed,
        out_specs=P("row", "col", None, None, None),
        check_vma=False,
    )
```

```python
import functools

import jax
import jax.numpy as jnp
from jax import lax
from jax.experimental import pallas as pl
from jax.experimental.pallas import tpu as pltpu
from jax.sharding import PartitionSpec as P

PANELS = 4
FIRST = 3
EARLY = 2
GROUP = 32
CHUNK = 16
SUB = 8
STRIPS = GROUP // SUB
F32 = jnp.float32
BF16 = jnp.bfloat16
HIGHEST = lax.Precision.HIGHEST
HBM = pl.BlockSpec(memory_space=pl.ANY)
SMEM = pl.BlockSpec(memory_space=pltpu.SMEM)
VMEM = pl.BlockSpec(memory_space=pltpu.VMEM)


def find(ids, rows, place, slots):
    me, column = lax.axis_index("row"), lax.axis_index("col")
    places = lax.broadcasted_iota(jnp.int32, (1, slots), 1)
    hit = (ids[1:2, :] == column) & (ids[0:1, :] == rows[place, me])
    return jnp.max(jnp.where(hit, places, -1))


def extract_kernel(col_devices, ids, rows, values, panel, head, table, sems):
    slots, count = values.shape[0], rows.shape[0]
    groups = rows.shape[1] // col_devices
    me = lax.axis_index("row")
    column = lax.axis_index("col")
    copies, present = [], []
    for place in range(count):
        found = find(ids, rows, place, slots)
        present.append(found >= 0)
        copy = pltpu.make_async_copy(
            values.at[jnp.maximum(found, 0)], panel.at[place], sems.at[place]
        )
        copy.start()
        copies.append(copy)
    row_ids, col_ids = ids[0:1, :], ids[1:2, :]
    row_place = jnp.full((1, slots), -1, jnp.int32)
    col_place = jnp.full((1, slots), -1, jnp.int32)
    for place in range(count):
        row_place = jnp.where(row_ids == rows[place, me], place, row_place)
        for group in range(groups):
            known = rows[place, column + group * col_devices]
            col_place = jnp.where(col_ids == known, group * count + place, col_place)
    both = (row_place >= 0) & (col_place >= 0)
    kind = jnp.where(row_ids < 0, 0, jnp.where(both, jnp.where(col_ids < PANELS, 2, 3), 1))
    table[0:1, :] = kind
    table[1:2, :] = jnp.maximum(row_place, 0)
    table[2:3, :] = jnp.maximum(col_place, 0)
    for place, copy in enumerate(copies):
        copy.wait()
        block = jnp.where(present[place], panel[place], 0.0)
        panel[place] = block
        if place == 0:
            head[0] = block


def extract(ids, rows, values, col_devices):
    slots, size, _ = values.shape
    count = rows.shape[0]
    return pl.pallas_call(
        functools.partial(extract_kernel, col_devices),
        name="extract",
        in_specs=[VMEM, SMEM, HBM],
        out_specs=[VMEM, VMEM, VMEM],
        out_shape=[
            jax.ShapeDtypeStruct((count, size, size), F32),
            jax.ShapeDtypeStruct((1, size, size), F32),
            jax.ShapeDtypeStruct((3, slots), jnp.int32),
        ],
        scratch_shapes=[pltpu.SemaphoreType.DMA((count,))],
    )(ids, rows, values)


def one_row(strip, place):
    return jnp.broadcast_to(strip[place : place + 1, :], strip.shape)


def eliminate(upper, extra, start):
    width = upper[0].shape[1]
    sublane = lax.broadcasted_iota(jnp.int32, (SUB, width), 0)
    scale = [jnp.zeros((SUB, width), F32)] * STRIPS
    for first in range(0, GROUP, CHUNK):
        chunk = range(first, first + CHUNK)
        cols = {
            t: {
                q: jnp.broadcast_to(upper[q][:, start + t : start + t + 1], (SUB, width))
                for q in range(t // SUB, STRIPS)
            }
            for t in chunk
        }
        for t in chunk:
            strip, place = divmod(t, SUB)
            pivot = one_row(cols[t][strip], place)
            reciprocal = 1.0 / pivot
            scale[strip] = jnp.where(sublane == place, lax.rsqrt(pivot), scale[strip])
            factor = {q: cols[t][q] * reciprocal for q in range(strip, STRIPS)}
            factor[strip] = jnp.where(sublane > place, factor[strip], 0.0)
            for u in chunk[t + 1 - first :]:
                entry = one_row(cols[t][u // SUB], u % SUB)
                for q in range(u // SUB, STRIPS):
                    cols[u][q] = cols[u][q] - factor[q] * entry
            pivot_upper = one_row(upper[strip], place)
            pivot_extra = one_row(extra[strip], place)
            for q in range(strip, STRIPS):
                upper[q] = upper[q] - factor[q] * pivot_upper
                extra[q] = extra[q] - factor[q] * pivot_extra
    upper = jnp.concatenate([upper[q] * scale[q] for q in range(STRIPS)], axis=0)
    extra = jnp.concatenate([extra[q] * scale[q] for q in range(STRIPS)], axis=0)
    return upper, extra


def exact(a, b):
    return jnp.dot(a, b, precision=HIGHEST, preferred_element_type=F32)


def exact_t(a, b):
    return lax.dot_general(
        a, b, (((1,), (1,)), ((), ())), precision=HIGHEST, preferred_element_type=F32
    )


def factor_block(block, work, extra_work):
    size = block.shape[0]
    row_place = lax.broadcasted_iota(jnp.int32, (size, size), 0)
    col_place = lax.broadcasted_iota(jnp.int32, (size, size), 1)
    work[...] = block
    extra_work[...] = jnp.where(row_place == col_place, 1.0, 0.0)
    uppers, extras = [], []
    for start in range(0, size, GROUP):
        strips = [pl.ds(start + q * SUB, SUB) for q in range(STRIPS)]
        upper = [work[s, :] for s in strips]
        extra = [extra_work[s, :] for s in strips]
        upper, extra = eliminate(upper, extra, start)
        uppers.append(upper)
        extras.append(extra)
        end = start + GROUP
        if end < size:
            left = upper[:, end:].T
            work[end:, :] = work[end:, :] - exact(left, upper)
            extra_work[end:, :] = extra_work[end:, :] - exact(left, extra)
    upper = jnp.concatenate(uppers, axis=0)
    inverse = jnp.where(row_place >= col_place, jnp.concatenate(extras, axis=0), 0.0)
    return jnp.where(row_place <= col_place, upper, 0.0), inverse


def halves(x):
    high = x.astype(BF16)
    return high, (x - high.astype(F32)).astype(BF16)


def at(row, col):
    return row * (row + 1) // 2 + col


def factor_steps(steps, lead, inverse, work, extra_work):
    for k in steps:
        upper, inv = factor_block(lead[at(k, k)], work, extra_work)
        lead[at(k, k)] = upper.T
        for i in range(k + 1, PANELS):
            lead[at(i, k)] = exact_t(lead[at(i, k)], inv)
        for i in range(k + 1, PANELS):
            for j in range(k + 1, i + 1):
                lead[at(i, j)] = lead[at(i, j)] - exact_t(lead[at(i, k)], lead[at(j, k)])
        inverse[at(k, k)] = inv
        for j in range(k):
            total = exact(lead[at(k, j)], inverse[at(j, j)])
            for m in range(j + 1, k):
                total = total + exact(lead[at(k, m)], inverse[at(m, j)])
            inverse[at(k, j)] = -exact(inv, total)


def first_kernel(near, across, lead, inverse, work, extra_work):
    me = lax.axis_index("row")
    column = lax.axis_index("col")
    for row in range(PANELS):
        for col in range(row + 1):
            flip_x = ((me // 2) % 2) ^ (row // 2)
            flip_core = (me % 2) ^ (row % 2)
            place = column ^ col

            @pl.when(flip_core == 0)
            def _():
                lead[at(row, col)] = near[flip_x, place]

            @pl.when(flip_core == 1)
            def _():
                lead[at(row, col)] = across[flip_x, place]

    factor_steps(range(FIRST), lead, inverse, work, extra_work)


def second_kernel(
    lead_in, inverse_in, factor, inv_hi, inv_lo, lead, inverse, work, extra_work
):
    size = work.shape[0]
    done = at(FIRST, 0)
    lead[...] = lead_in[...]
    inverse[:done] = inverse_in[...]
    factor_steps(range(FIRST, PANELS), lead, inverse, work, extra_work)
    zero = jnp.zeros((size, size), BF16)
    for i in range(PANELS):
        for j in range(PANELS):
            rows, cols = slice(i * size, (i + 1) * size), slice(j * size, (j + 1) * size)
            hi, lo = halves(inverse[at(i, j)]) if j <= i else (zero, zero)
            inv_hi[rows, cols], inv_lo[rows, cols] = hi, lo
    row = jnp.minimum(lax.axis_index("row"), PANELS - 1)
    factor[...] = lead[at(row, jnp.minimum(lax.axis_index("col"), row))]


FACTOR_COST = pl.CostEstimate(flops=2**33, bytes_accessed=2**24, transcendentals=0)


def factor_first(near, across):
    size = near.shape[-1]
    return pl.pallas_call(
        first_kernel,
        name="factor_first",
        in_specs=[VMEM, VMEM],
        out_specs=[VMEM, VMEM],
        out_shape=[
            jax.ShapeDtypeStruct((at(PANELS, 0), size, size), F32),
            jax.ShapeDtypeStruct((at(FIRST, 0), size, size), F32),
        ],
        scratch_shapes=[pltpu.VMEM((size, size), F32), pltpu.VMEM((size, size), F32)],
        compiler_params=pltpu.CompilerParams(vmem_limit_bytes=16 * 2**20),
        cost_estimate=FACTOR_COST,
    )(near, across)


def factor_second(lead, inverse):
    size = lead.shape[-1]
    width = PANELS * size
    return pl.pallas_call(
        second_kernel,
        name="factor_second",
        in_specs=[VMEM, VMEM],
        out_specs=[VMEM, VMEM, VMEM],
        out_shape=[
            jax.ShapeDtypeStruct((size, size), F32),
            jax.ShapeDtypeStruct((width, width), BF16),
            jax.ShapeDtypeStruct((width, width), BF16),
        ],
        scratch_shapes=[
            pltpu.VMEM((at(PANELS, 0), size, size), F32),
            pltpu.VMEM((at(PANELS, 0), size, size), F32),
            pltpu.VMEM((size, size), F32),
            pltpu.VMEM((size, size), F32),
        ],
        compiler_params=pltpu.CompilerParams(vmem_limit_bytes=16 * 2**20),
        cost_estimate=FACTOR_COST,
    )(lead, inverse)


def dot3_t(a, b):
    dims = (((1,), (1,)), ((), ()))
    dot = functools.partial(lax.dot_general, dimension_numbers=dims, preferred_element_type=F32)
    return dot(a[0], b[0]) + (dot(a[0], b[1]) + dot(a[1], b[0]))


def spread(column, place):
    return place ^ (2 * (column % 2))


def update_kernel(plan, table, *refs):
    row_devices, count, col_devices = plan
    groups = row_devices // col_devices
    refs = list(refs)
    panels = [refs.pop(0) for _ in range(col_devices)]
    near = [refs.pop(0) for _ in range(row_devices // 2)]
    across = refs.pop(0)
    factor, inv_hi, inv_lo, values, out = [refs.pop(0) for _ in range(5)]
    raw, high, low, product, column_blocks, slots_in, sems, io_sems = refs
    slots, size, _ = values.shape
    own_rows = count * size
    far_rows = groups * own_rows
    me = lax.axis_index("row")
    column = lax.axis_index("col")

    def lanes_of(col):
        return pl.ds(pl.multiple_of(jnp.minimum(col, PANELS - 1) * size, size), size)

    twice = (me ^ column) % col_devices == 0
    for p in range(col_devices):
        col = column ^ p

        @pl.when((col < PANELS) & jnp.logical_not(twice))
        def _():
            target = raw.at[:own_rows, lanes_of(col)]
            pltpu.make_async_copy(panels[p], target, sems.at[0]).start()

    for flip in range(row_devices):
        holder = me ^ flip
        group, col = holder // col_devices, spread(column, holder % col_devices)
        if flip % 2 == 0:
            source = near[flip // 2]
        else:
            source = across.at[flip // 2 * own_rows : (flip // 2 + 1) * own_rows]

        @pl.when(twice & (col < PANELS) & (group == me // col_devices))
        def _():
            target = raw.at[:own_rows, lanes_of(col)]
            pltpu.make_async_copy(source, target, sems.at[0]).start()

    for flip in range(row_devices):
        holder = me ^ flip
        group, col = holder // col_devices, spread(column, holder % col_devices)
        if flip % 2 == 0:
            source = near[flip // 2]
        else:
            source = across.at[flip // 2 * own_rows : (flip // 2 + 1) * own_rows]

        @pl.when(col < PANELS)
        def _():
            start = pl.multiple_of((group + 1) * own_rows, own_rows)
            target = raw.at[pl.ds(start, own_rows), lanes_of(col)]
            pltpu.make_async_copy(source, target, sems.at[1]).start()

    load = pltpu.make_async_copy(values, slots_in, io_sems.at[0])
    load.start()
    half = PANELS * size // 2
    for part in range(groups + 1):
        if part < 2:
            arrived = raw.at[:own_rows, :] if part == 0 else raw.at[own_rows:, :]
            pltpu.make_async_copy(arrived, arrived, sems.at[part]).wait()
        rows = pl.ds(part * own_rows, own_rows)
        hi, lo = halves(raw[rows, :])
        first = dot3_t(
            (hi[:, :half], lo[:, :half]), (inv_hi[:half, :half], inv_lo[:half, :half])
        )
        second = dot3_t((hi, lo), (inv_hi[half:, :], inv_lo[half:, :]))
        if part == 0:
            raw[rows, :half], raw[rows, half:] = first, second
        high[rows, :half], low[rows, :half] = halves(first)
        high[rows, half:], low[rows, half:] = halves(second)
    load.wait()
    own = pl.ds(0, own_rows)
    for start in range(0, far_rows, 2 * size):
        rows = pl.ds(own_rows + start, 2 * size)
        result = dot3_t((high[own, :], low[own, :]), (high[rows, :], low[rows, :]))
        for place in range(count):
            for side in range(2):
                product[place, start // size + side] = result[
                    place * size : (place + 1) * size, side * size : (side + 1) * size
                ]
    lanes = lanes_of(column)
    for place in range(count):
        solved_block = raw[place * size : (place + 1) * size, lanes]
        if place == 0:
            solved_block = jnp.where(me < PANELS, factor[...], solved_block)
        column_blocks[place] = solved_block

    def finish(slot, carry):
        kind, row, col = table[0, slot], table[1, slot], table[2, slot]
        old = slots_in[slot]
        new = jnp.where(kind == 3, old - product[row, col], jnp.where(kind == 1, old, 0.0))
        slots_in[slot] = jnp.where(kind == 2, column_blocks[row], new)
        pltpu.make_async_copy(slots_in.at[slot], out.at[slot], io_sems.at[1]).start()
        return carry

    lax.fori_loop(0, slots, finish, 0, unroll=4)
    pltpu.make_async_copy(slots_in, out, io_sems.at[1]).wait()


def update(table, panels, near, across, solved_lead, values, row_devices):
    slots, size, _ = values.shape
    col_devices, count = len(panels), panels[0].shape[0]
    groups = row_devices // col_devices
    flat = [x.reshape(-1, size) for x in (*panels, *near, across)]
    width = PANELS * size
    rows = (groups + 1) * count * size
    return pl.pallas_call(
        functools.partial(update_kernel, (row_devices, count, col_devices)),
        name="update",
        in_specs=[SMEM] + [HBM] * len(flat) + [VMEM, VMEM, VMEM, HBM],
        out_specs=HBM,
        out_shape=jax.ShapeDtypeStruct(values.shape, F32),
        scratch_shapes=[
            pltpu.VMEM((rows, width), F32),
            pltpu.VMEM((rows, width), BF16),
            pltpu.VMEM((rows, width), BF16),
            pltpu.VMEM((count, groups * count, size, size), F32),
            pltpu.VMEM((count, size, size), F32),
            pltpu.VMEM((slots, size, size), F32),
            pltpu.SemaphoreType.DMA((2,)),
            pltpu.SemaphoreType.DMA((2,)),
        ],
        compiler_params=pltpu.CompilerParams(vmem_limit_bytes=24 * 2**20),
    )(table, *flat, *solved_lead, values)


def body(values, block_ids, coupled_rows):
    row_devices, col_devices = lax.axis_size("row"), lax.axis_size("col")
    every_row, every_col = range(row_devices), range(col_devices)
    me = lax.axis_index("row")
    slot_values = values[0, 0]
    rows = coupled_rows.T

    def send(x, flip, keep=lambda r, c: True):
        pairs = [
            (r * col_devices + c, (r ^ flip) * col_devices + c)
            for r in every_row
            for c in every_col
            if keep(r, c)
        ]
        return lax.ppermute(x, ("row", "col"), pairs)

    def over_col(x, keep=lambda r, c: True):
        got = [x]
        for p in range(1, col_devices):
            pairs = [
                (r * col_devices + c, r * col_devices + (c ^ p))
                for r in every_row
                for c in range(PANELS)
                if keep(r, c ^ p)
            ]
            got.append(lax.ppermute(x, ("row", "col"), pairs))
        return got

    panel, head, table = extract(block_ids[0, 0].T, rows, slot_values, col_devices)

    block = jnp.where(me < PANELS, head, 0.0)
    step = PANELS
    while step < row_devices:
        block = block + send(block, step, lambda r, c: r < step)
        step *= 2
    blocks = over_col(block)

    pairs = [
        ((q + a) * col_devices + b, (q + spread(a, b)) * col_devices + a)
        for q in range(0, row_devices, col_devices)
        for a in every_col
        for b in range(PANELS)
    ]
    blocks, panel = lax.optimization_barrier((blocks, panel))
    turned = lax.ppermute(panel, ("row", "col"), pairs)

    panels = over_col(panel, lambda r, c: (r ^ c) % col_devices != 0)

    mine = jnp.concatenate(blocks, axis=0)
    beside, panels[EARLY], turned = lax.optimization_barrier(
        (send(mine, 2), panels[EARLY], turned)
    )
    near_lead = jnp.stack([mine, beside])
    across_lead = send(near_lead, 1)
    near = [turned if flip == 0 else send(turned, flip) for flip in range(0, row_devices, 2)]
    begun = factor_first(near_lead, across_lead)
    late = [panels[p] for p in range(col_devices) if p != EARLY]
    near, late, begun = lax.optimization_barrier((near, late, begun))
    panels = late[:EARLY] + [panels[EARLY]] + late[EARLY:]
    across = send(jnp.concatenate(near, axis=0), 1)
    solved_lead = factor_second(*begun)

    result = update(table, panels, near, across, solved_lead, slot_values, row_devices)
    return result[None, None]


def solution(mesh):
    placed = (P("row", "col", None, None, None), P("row", "col", None, None), P())
    return jax.shard_map(
        body,
        mesh=mesh,
        in_specs=placed,
        out_specs=P("row", "col", None, None, None),
        check_vma=False,
    )
```

```python
import functools

import jax
import jax.numpy as jnp
from jax import lax
from jax.experimental import pallas as pl
from jax.experimental.pallas import tpu as pltpu
from jax.sharding import PartitionSpec as P

PANELS = 4
FIRST = 3
EARLY = 2
GROUP = 32
CHUNK = 16
SUB = 8
STRIPS = GROUP // SUB
F32 = jnp.float32
BF16 = jnp.bfloat16
HIGHEST = lax.Precision.HIGHEST
HBM = pl.BlockSpec(memory_space=pl.ANY)
SMEM = pl.BlockSpec(memory_space=pltpu.SMEM)
VMEM = pl.BlockSpec(memory_space=pltpu.VMEM)


def find(ids, rows, place, slots):
    me, column = lax.axis_index("row"), lax.axis_index("col")
    places = lax.broadcasted_iota(jnp.int32, (1, slots), 1)
    hit = (ids[1:2, :] == column) & (ids[0:1, :] == rows[place, me])
    return jnp.max(jnp.where(hit, places, -1))


def extract_kernel(col_devices, ids, rows, values, panel, head, table, sems):
    slots, count = values.shape[0], rows.shape[0]
    groups = rows.shape[1] // col_devices
    me = lax.axis_index("row")
    column = lax.axis_index("col")
    copies, present = [], []
    for place in range(count):
        found = find(ids, rows, place, slots)
        present.append(found >= 0)
        copy = pltpu.make_async_copy(
            values.at[jnp.maximum(found, 0)], panel.at[place], sems.at[place]
        )
        copy.start()
        copies.append(copy)
    row_ids, col_ids = ids[0:1, :], ids[1:2, :]
    row_place = jnp.full((1, slots), -1, jnp.int32)
    col_place = jnp.full((1, slots), -1, jnp.int32)
    for place in range(count):
        row_place = jnp.where(row_ids == rows[place, me], place, row_place)
        for group in range(groups):
            known = rows[place, column + group * col_devices]
            col_place = jnp.where(col_ids == known, group * count + place, col_place)
    both = (row_place >= 0) & (col_place >= 0)
    kind = jnp.where(row_ids < 0, 0, jnp.where(both, jnp.where(col_ids < PANELS, 2, 3), 1))
    table[0:1, :] = kind
    table[1:2, :] = jnp.maximum(row_place, 0)
    table[2:3, :] = jnp.maximum(col_place, 0)
    for place, copy in enumerate(copies):
        copy.wait()
        block = jnp.where(present[place], panel[place], 0.0)
        panel[place] = block
        if place == 0:
            head[0] = block


def extract(ids, rows, values, col_devices):
    slots, size, _ = values.shape
    count = rows.shape[0]
    return pl.pallas_call(
        functools.partial(extract_kernel, col_devices),
        name="extract",
        in_specs=[VMEM, SMEM, HBM],
        out_specs=[VMEM, VMEM, VMEM],
        out_shape=[
            jax.ShapeDtypeStruct((count, size, size), F32),
            jax.ShapeDtypeStruct((1, size, size), F32),
            jax.ShapeDtypeStruct((3, slots), jnp.int32),
        ],
        scratch_shapes=[pltpu.SemaphoreType.DMA((count,))],
    )(ids, rows, values)


def one_row(strip, place):
    return jnp.broadcast_to(strip[place : place + 1, :], strip.shape)


def eliminate(upper, extra, start):
    width = upper[0].shape[1]
    sublane = lax.broadcasted_iota(jnp.int32, (SUB, width), 0)
    scale = [jnp.zeros((SUB, width), F32)] * STRIPS
    for first in range(0, GROUP, CHUNK):
        chunk = range(first, first + CHUNK)
        cols = {
            t: {
                q: jnp.broadcast_to(upper[q][:, start + t : start + t + 1], (SUB, width))
                for q in range(t // SUB, STRIPS)
            }
            for t in chunk
        }
        for t in chunk:
            strip, place = divmod(t, SUB)
            pivot = one_row(cols[t][strip], place)
            reciprocal = 1.0 / pivot
            scale[strip] = jnp.where(sublane == place, lax.rsqrt(pivot), scale[strip])
            factor = {q: cols[t][q] * reciprocal for q in range(strip, STRIPS)}
            factor[strip] = jnp.where(sublane > place, factor[strip], 0.0)
            for u in chunk[t + 1 - first :]:
                entry = one_row(cols[t][u // SUB], u % SUB)
                for q in range(u // SUB, STRIPS):
                    cols[u][q] = cols[u][q] - factor[q] * entry
            pivot_upper = one_row(upper[strip], place)
            pivot_extra = one_row(extra[strip], place)
            for q in range(strip, STRIPS):
                upper[q] = upper[q] - factor[q] * pivot_upper
                extra[q] = extra[q] - factor[q] * pivot_extra
    upper = jnp.concatenate([upper[q] * scale[q] for q in range(STRIPS)], axis=0)
    extra = jnp.concatenate([extra[q] * scale[q] for q in range(STRIPS)], axis=0)
    return upper, extra


def exact(a, b):
    return jnp.dot(a, b, precision=HIGHEST, preferred_element_type=F32)


def exact_t(a, b):
    return lax.dot_general(
        a, b, (((1,), (1,)), ((), ())), precision=HIGHEST, preferred_element_type=F32
    )


def factor_block(block, work, extra_work):
    size = block.shape[0]
    row_place = lax.broadcasted_iota(jnp.int32, (size, size), 0)
    col_place = lax.broadcasted_iota(jnp.int32, (size, size), 1)
    work[...] = block
    extra_work[...] = jnp.where(row_place == col_place, 1.0, 0.0)
    uppers, extras = [], []
    for start in range(0, size, GROUP):
        strips = [pl.ds(start + q * SUB, SUB) for q in range(STRIPS)]
        upper = [work[s, :] for s in strips]
        extra = [extra_work[s, :] for s in strips]
        upper, extra = eliminate(upper, extra, start)
        uppers.append(upper)
        extras.append(extra)
        end = start + GROUP
        if end < size:
            left = upper[:, end:].T
            work[end:, :] = work[end:, :] - exact(left, upper)
            extra_work[end:, :] = extra_work[end:, :] - exact(left, extra)
    upper = jnp.concatenate(uppers, axis=0)
    inverse = jnp.where(row_place >= col_place, jnp.concatenate(extras, axis=0), 0.0)
    return jnp.where(row_place <= col_place, upper, 0.0), inverse


def halves(x):
    high = x.astype(BF16)
    return high, (x - high.astype(F32)).astype(BF16)


def at(row, col):
    return row * (row + 1) // 2 + col


def factor_steps(steps, lead, inverse, work, extra_work):
    for k in steps:
        upper, inv = factor_block(lead[at(k, k)], work, extra_work)
        lead[at(k, k)] = upper.T
        for i in range(k + 1, PANELS):
            lead[at(i, k)] = exact_t(lead[at(i, k)], inv)
        for i in range(k + 1, PANELS):
            for j in range(k + 1, i + 1):
                lead[at(i, j)] = lead[at(i, j)] - exact_t(lead[at(i, k)], lead[at(j, k)])
        inverse[at(k, k)] = inv
        for j in range(k):
            total = exact(lead[at(k, j)], inverse[at(j, j)])
            for m in range(j + 1, k):
                total = total + exact(lead[at(k, m)], inverse[at(m, j)])
            inverse[at(k, j)] = -exact(inv, total)


def first_kernel(near, across, lead, inverse, work, extra_work):
    me = lax.axis_index("row")
    column = lax.axis_index("col")
    for row in range(PANELS):
        for col in range(row + 1):
            flip_x = ((me // 2) % 2) ^ (row // 2)
            flip_core = (me % 2) ^ (row % 2)
            place = column ^ col

            @pl.when(flip_core == 0)
            def _():
                lead[at(row, col)] = near[flip_x, place]

            @pl.when(flip_core == 1)
            def _():
                lead[at(row, col)] = across[flip_x, place]

    factor_steps(range(FIRST), lead, inverse, work, extra_work)


def second_kernel(
    lead_in, inverse_in, factor, inv_hi, inv_lo, lead, inverse, work, extra_work
):
    size = work.shape[0]
    done = at(FIRST, 0)
    lead[...] = lead_in[...]
    inverse[:done] = inverse_in[...]
    factor_steps(range(FIRST, PANELS), lead, inverse, work, extra_work)
    zero = jnp.zeros((size, size), BF16)
    for i in range(PANELS):
        for j in range(PANELS):
            rows, cols = slice(i * size, (i + 1) * size), slice(j * size, (j + 1) * size)
            hi, lo = halves(inverse[at(i, j)]) if j <= i else (zero, zero)
            inv_hi[rows, cols], inv_lo[rows, cols] = hi, lo
    row = jnp.minimum(lax.axis_index("row"), PANELS - 1)
    factor[...] = lead[at(row, jnp.minimum(lax.axis_index("col"), row))]


FACTOR_COST = pl.CostEstimate(flops=2**33, bytes_accessed=2**24, transcendentals=0)


def factor_first(near, across):
    size = near.shape[-1]
    return pl.pallas_call(
        first_kernel,
        name="factor_first",
        in_specs=[VMEM, VMEM],
        out_specs=[VMEM, VMEM],
        out_shape=[
            jax.ShapeDtypeStruct((at(PANELS, 0), size, size), F32),
            jax.ShapeDtypeStruct((at(FIRST, 0), size, size), F32),
        ],
        scratch_shapes=[pltpu.VMEM((size, size), F32), pltpu.VMEM((size, size), F32)],
        compiler_params=pltpu.CompilerParams(vmem_limit_bytes=16 * 2**20),
        cost_estimate=FACTOR_COST,
    )(near, across)


def factor_second(lead, inverse):
    size = lead.shape[-1]
    width = PANELS * size
    return pl.pallas_call(
        second_kernel,
        name="factor_second",
        in_specs=[VMEM, VMEM],
        out_specs=[VMEM, VMEM, VMEM],
        out_shape=[
            jax.ShapeDtypeStruct((size, size), F32),
            jax.ShapeDtypeStruct((width, width), BF16),
            jax.ShapeDtypeStruct((width, width), BF16),
        ],
        scratch_shapes=[
            pltpu.VMEM((at(PANELS, 0), size, size), F32),
            pltpu.VMEM((at(PANELS, 0), size, size), F32),
            pltpu.VMEM((size, size), F32),
            pltpu.VMEM((size, size), F32),
        ],
        compiler_params=pltpu.CompilerParams(vmem_limit_bytes=16 * 2**20),
        cost_estimate=FACTOR_COST,
    )(lead, inverse)


def dot3_t(a, b):
    dims = (((1,), (1,)), ((), ()))
    dot = functools.partial(lax.dot_general, dimension_numbers=dims, preferred_element_type=F32)
    return dot(a[0], b[0]) + (dot(a[0], b[1]) + dot(a[1], b[0]))


def spread(column, place):
    return place ^ (2 * (column % 2))


def update_kernel(plan, table, *refs):
    row_devices, count, col_devices = plan
    groups = row_devices // col_devices
    refs = list(refs)
    panels = [refs.pop(0) for _ in range(col_devices)]
    near = [refs.pop(0) for _ in range(row_devices // 2)]
    across = refs.pop(0)
    factor, inv_hi, inv_lo, values, out = [refs.pop(0) for _ in range(5)]
    raw, high, low, product, column_blocks, slots_in, sems, io_sems = refs
    slots, size, _ = values.shape
    own_rows = count * size
    far_rows = groups * own_rows
    me = lax.axis_index("row")
    column = lax.axis_index("col")

    def lanes_of(col):
        return pl.ds(pl.multiple_of(jnp.minimum(col, PANELS - 1) * size, size), size)

    twice = (me ^ column) % col_devices == 0
    for p in range(col_devices):
        col = column ^ p

        @pl.when((col < PANELS) & jnp.logical_not(twice))
        def _():
            target = raw.at[:own_rows, lanes_of(col)]
            pltpu.make_async_copy(panels[p], target, sems.at[0]).start()

    for flip in range(row_devices):
        holder = me ^ flip
        group, col = holder // col_devices, spread(column, holder % col_devices)
        if flip % 2 == 0:
            source = near[flip // 2]
        else:
            source = across.at[flip // 2 * own_rows : (flip // 2 + 1) * own_rows]

        @pl.when(twice & (col < PANELS) & (group == me // col_devices))
        def _():
            target = raw.at[:own_rows, lanes_of(col)]
            pltpu.make_async_copy(source, target, sems.at[0]).start()

    for flip in range(row_devices):
        holder = me ^ flip
        group, col = holder // col_devices, spread(column, holder % col_devices)
        if flip % 2 == 0:
            source = near[flip // 2]
        else:
            source = across.at[flip // 2 * own_rows : (flip // 2 + 1) * own_rows]

        @pl.when(col < PANELS)
        def _():
            start = pl.multiple_of((group + 1) * own_rows, own_rows)
            target = raw.at[pl.ds(start, own_rows), lanes_of(col)]
            pltpu.make_async_copy(source, target, sems.at[1]).start()

    load = pltpu.make_async_copy(values, slots_in, io_sems.at[0])
    load.start()
    half = PANELS * size // 2
    for part in range(groups + 1):
        if part < 2:
            arrived = raw.at[:own_rows, :] if part == 0 else raw.at[own_rows:, :]
            pltpu.make_async_copy(arrived, arrived, sems.at[part]).wait()
        rows = pl.ds(part * own_rows, own_rows)
        hi, lo = halves(raw[rows, :])
        first = dot3_t(
            (hi[:, :half], lo[:, :half]), (inv_hi[:half, :half], inv_lo[:half, :half])
        )
        second = dot3_t((hi, lo), (inv_hi[half:, :], inv_lo[half:, :]))
        if part == 0:
            raw[rows, :half], raw[rows, half:] = first, second
        high[rows, :half], low[rows, :half] = halves(first)
        high[rows, half:], low[rows, half:] = halves(second)
    load.wait()
    own = pl.ds(0, own_rows)
    for start in range(0, far_rows, 2 * size):
        rows = pl.ds(own_rows + start, 2 * size)
        result = dot3_t((high[own, :], low[own, :]), (high[rows, :], low[rows, :]))
        for place in range(count):
            for side in range(2):
                product[place, start // size + side] = result[
                    place * size : (place + 1) * size, side * size : (side + 1) * size
                ]
    lanes = lanes_of(column)
    for place in range(count):
        solved_block = raw[place * size : (place + 1) * size, lanes]
        if place == 0:
            solved_block = jnp.where(me < PANELS, factor[...], solved_block)
        column_blocks[place] = solved_block

    def finish(slot, carry):
        kind, row, col = table[0, slot], table[1, slot], table[2, slot]
        old = slots_in[slot]
        new = jnp.where(kind == 3, old - product[row, col], jnp.where(kind == 1, old, 0.0))
        slots_in[slot] = jnp.where(kind == 2, column_blocks[row], new)
        pltpu.make_async_copy(slots_in.at[slot], out.at[slot], io_sems.at[1]).start()
        return carry

    lax.fori_loop(0, slots, finish, 0, unroll=4)
    pltpu.make_async_copy(slots_in, out, io_sems.at[1]).wait()


def update(table, panels, near, across, solved_lead, values, row_devices):
    slots, size, _ = values.shape
    col_devices, count = len(panels), panels[0].shape[0]
    groups = row_devices // col_devices
    flat = [x.reshape(-1, size) for x in (*panels, *near, across)]
    width = PANELS * size
    rows = (groups + 1) * count * size
    return pl.pallas_call(
        functools.partial(update_kernel, (row_devices, count, col_devices)),
        name="update",
        in_specs=[SMEM] + [HBM] * len(flat) + [VMEM, VMEM, VMEM, HBM],
        out_specs=HBM,
        out_shape=jax.ShapeDtypeStruct(values.shape, F32),
        scratch_shapes=[
            pltpu.VMEM((rows, width), F32),
            pltpu.VMEM((rows, width), BF16),
            pltpu.VMEM((rows, width), BF16),
            pltpu.VMEM((count, groups * count, size, size), F32),
            pltpu.VMEM((count, size, size), F32),
            pltpu.VMEM((slots, size, size), F32),
            pltpu.SemaphoreType.DMA((2,)),
            pltpu.SemaphoreType.DMA((2,)),
        ],
        compiler_params=pltpu.CompilerParams(vmem_limit_bytes=24 * 2**20),
    )(table, *flat, *solved_lead, values)


def body(values, block_ids, coupled_rows):
    row_devices, col_devices = lax.axis_size("row"), lax.axis_size("col")
    every_row, every_col = range(row_devices), range(col_devices)
    me = lax.axis_index("row")
    slot_values = values[0, 0]
    rows = coupled_rows.T

    def send(x, flip, keep=lambda r, c: True):
        pairs = [
            (r * col_devices + c, (r ^ flip) * col_devices + c)
            for r in every_row
            for c in every_col
            if keep(r, c)
        ]
        return lax.ppermute(x, ("row", "col"), pairs)

    def over_col(x, keep=lambda r, c: True):
        got = [x]
        for p in range(1, col_devices):
            pairs = [
                (r * col_devices + c, r * col_devices + (c ^ p))
                for r in every_row
                for c in range(PANELS)
                if keep(r, c ^ p)
            ]
            got.append(lax.ppermute(x, ("row", "col"), pairs))
        return got

    panel, head, table = extract(block_ids[0, 0].T, rows, slot_values, col_devices)

    block = jnp.where(me < PANELS, head, 0.0)
    step = PANELS
    while step < row_devices:
        block = block + send(block, step, lambda r, c: r < step)
        step *= 2
    blocks = over_col(block)

    pairs = [
        ((q + a) * col_devices + b, (q + spread(a, b)) * col_devices + a)
        for q in range(0, row_devices, col_devices)
        for a in every_col
        for b in range(PANELS)
    ]
    blocks, panel = lax.optimization_barrier((blocks, panel))
    turned = lax.ppermute(panel, ("row", "col"), pairs)

    panels = over_col(panel, lambda r, c: (r ^ c) % col_devices != 0)

    mine = jnp.concatenate(blocks, axis=0)
    panels[EARLY], beside, turned = lax.optimization_barrier(
        (panels[EARLY], send(mine, 2), turned)
    )
    near_lead = jnp.stack([mine, beside])
    across_lead = send(near_lead, 1)
    near = [turned if flip == 0 else send(turned, flip) for flip in range(0, row_devices, 2)]
    begun = factor_first(near_lead, across_lead)
    late = [panels[p] for p in range(col_devices) if p != EARLY]
    near, late, begun = lax.optimization_barrier((near, late, begun))
    panels = late[:EARLY] + [panels[EARLY]] + late[EARLY:]
    across = send(jnp.concatenate(near, axis=0), 1)
    solved_lead = factor_second(*begun)

    result = update(table, panels, near, across, solved_lead, slot_values, row_devices)
    return result[None, None]


def solution(mesh):
    placed = (P("row", "col", None, None, None), P("row", "col", None, None), P())
    return jax.shard_map(
        body,
        mesh=mesh,
        in_specs=placed,
        out_specs=P("row", "col", None, None, None),
        check_vma=False,
    )
```
